256 devices in a mesh: rep: 32 (over z_lo, x, core), tp: 8 (over z_hi, y).
Axes of the slice: x: 4, y: 4, z: 8 (z_hi: 2, z_lo: 4; z = z_hi * 4 + z_lo), core: 2. Of those that a mesh axis runs over, the one named last changes fastest.
Arguments:
- tokens_in: bfloat16 [32768, 8192], P('rep', 'tp'), may hold values from -1300 to 1300
- gain: float32 [8192], P('tp'), may hold values from 0.1 to 1.9
- cotangent: bfloat16 [32768, 1024], P('rep', 'tp'), may hold values from -12 to 12
- local_weight: bfloat16 [32, 8192, 1024], P('rep', 'tp'), may hold values from -6 to 1030
- packed_codes: int32 [32, 8192, 512], P('rep', 'tp'), may hold values from 0 to 255
- code_scales: float32 [32, 8192, 8], P('rep', 'tp'), may hold values from 0.02 to 1
- global_weight: float32 [8, 1024, 1024], P('tp', 'rep'), may hold values from -6 to 6
- momentum: float32 [8, 1024, 1024], P('tp', 'rep'), may hold values from -3 to 3
Outputs:
- projected: bfloat16 [32768, 1024], P('rep', 'tp')
- grad_x: bfloat16 [32768, 8192], P('rep', 'tp')
- new_local: bfloat16 [32, 8192, 1024], P('rep', 'tp')
- new_global: float32 [8, 1024, 1024], P('tp', 'rep')
- new_momentum: float32 [8, 1024, 1024], P('tp', 'rep')
The draws below stay inside these ranges and needn't reach their ends.
All inputs are finite; a program needn't handle non-finite values.
Results may differ from the reference program's by a relative error of at most 0.017.
Values may be sent and summed in bfloat16 or wider, within the bound.
A program may use at most 64 MiB of HBM per device.

```python
import math
import jax
import jax.numpy as jnp
from jax import lax

D = 8192
KV_COLS = 1024
WORDS = 512
GROUPS = 8
D_DEV = 1024
TOK = 1024
TOKENS = 32768
N_REP = 32
N_TP = 8


def shared_uniform(key):
    return jax.random.uniform(key, (TOKENS, D), jnp.float32, 1e-06, 1.0 - 1e-06)


def feature_sets(key):
    order = jax.random.permutation(jax.random.fold_in(key, 91), D).astype(jnp.int32)
    slots = (8 * jnp.arange(KV_COLS, dtype=jnp.int32)[None, :] + jnp.arange(8, dtype=jnp.int32)[:, None]) % D
    return order[slots]


def draw_tokens_in(key, part):
    uniform_base = shared_uniform(key)
    key = jax.random.fold_in(key, 1)
    second, third = jax.random.split(key, 2)
    rising = 3.0 ** (jnp.arange(D, dtype=jnp.float32) / D)
    columns = rising * jnp.exp(jax.random.uniform(second, (D,), jnp.float32, 0.0, math.log(10.0)))
    rowscale = jnp.exp(jax.random.uniform(third, (TOKENS, 1), jnp.float32, 0.0, math.log(10.0)))
    base = jnp.clip(math.sqrt(2.0) * lax.erf_inv(2.0 * uniform_base - 1.0), -4.0, 4.0)
    return (base * rowscale * columns).astype(jnp.bfloat16)


def draw_cotangent(key, part):
    uniform_base = shared_uniform(key)
    chosen = feature_sets(key)
    key = jax.random.fold_in(key, 4)
    base = jnp.clip(math.sqrt(2.0) * lax.erf_inv(2.0 * uniform_base - 1.0), -4.0, 4.0)
    picked = [base[:, chosen[index]] for index in range(8)]
    summed = picked[0] + picked[1] + (picked[2] + picked[3]) + (picked[4] + picked[5] + (picked[6] + picked[7]))
    noise_part = jnp.clip(jax.random.normal(key, (TOKENS, KV_COLS), jnp.float32), -4.0, 4.0)
    return (0.9 / math.sqrt(8.0) * summed + 0.44 * noise_part).astype(jnp.bfloat16)


def draw_local_weight(key, part):
    chosen = feature_sets(key)
    key = jax.random.fold_in(key, 3)
    first, second = jax.random.split(key, 2)
    noise_part = jnp.clip(jax.random.normal(first, (N_REP, D, KV_COLS), jnp.float32), -6.0, 6.0)
    row_ids = jnp.arange(D, dtype=jnp.int32)[:, None]
    spike_mask = jnp.zeros((D, KV_COLS), jnp.float32)
    for index in range(8):
        spike_mask = spike_mask + (row_ids == chosen[index][None, :]).astype(jnp.float32)
    heights = math.sqrt(D / 8.0) * jax.random.uniform(second, (N_REP, 1, KV_COLS), jnp.float32, 0.5, 0.9)
    return (noise_part + spike_mask[None] * heights).astype(jnp.bfloat16)


def draw_code_scales(key, part):
    key = jax.random.fold_in(key, 2)
    position = jnp.arange(N_REP, dtype=jnp.float32) / max(N_REP - 1, 1)
    rising = (3.0 ** position)[:, None, None]
    base = jnp.exp(jax.random.uniform(key, (N_REP, D, GROUPS), jnp.float32, math.log(0.03), math.log(0.3)))
    return (base * rising).astype(jnp.float32)


def touch_ends(entries, own_key, least, top_value):
    spot = [jax.random.randint(jax.random.fold_in(own_key, axis), (), 0, length) for axis, length in enumerate(entries.shape)]
    longest = entries.shape.index(max(entries.shape))
    beside = spot[:longest] + [(spot[longest] + 1) % entries.shape[longest]] + spot[longest + 1:]
    return entries.at[tuple(spot)].set(least).at[tuple(beside)].set(top_value)


def block_levels(own_key, shape, cuts, low, high):
    def one(axis_at, shards_of):
        draws = jax.random.uniform(jax.random.fold_in(jax.random.fold_in(own_key, 6), axis_at), (shards_of,), jnp.float32, low / len(cuts), high / len(cuts))
        return jnp.repeat(jnp.exp(draws), shape[axis_at] // shards_of).reshape((-1,) + (1,) * (len(shape) - axis_at - 1))

    level = one(*cuts[0])
    for cut in cuts[1:]:
        level = level * one(*cut)
    return level


def noise(rng, dims, width, most, shards=(), kind=jnp.bfloat16):
    loudness = block_levels(rng, dims, shards, -0.22, 0.18) if shards else 1.0
    values = jax.random.normal(rng, dims, jnp.float32) * width * loudness
    return jnp.minimum(jnp.maximum(values, -most), most).astype(kind)


def setup_inputs(seed: int = 0) -> dict:
    streams_of = jax.random.split(jax.random.key(seed), 9)
    tokens_in = draw_tokens_in(jax.random.fold_in(streams_of[8], 71), 0)
    gain = jnp.clip(1.0 + 0.18 * jax.random.normal(streams_of[1], (D,), jnp.float32), 0.1, 1.9)
    cotangent = draw_cotangent(jax.random.fold_in(streams_of[8], 71), 0)
    local_weight = draw_local_weight(jax.random.fold_in(streams_of[8], 71), 0)
    packed_codes = touch_ends(jax.random.randint(streams_of[4], (N_REP, D, WORDS), 0, 256), jax.random.fold_in(streams_of[4], 1), 0, 255).astype(jnp.int32)
    code_scales = draw_code_scales(jax.random.fold_in(streams_of[8], 71), 0)
    global_weight = noise(streams_of[6], (N_TP, D_DEV, KV_COLS), 1.0, 6.0, ((0, 8), (1, 32)), jnp.float32)
    momentum = noise(streams_of[7], (N_TP, D_DEV, KV_COLS), 0.5, 3.0, ((0, 8), (1, 32)), jnp.float32)
    return dict(tokens_in=tokens_in, gain=gain, cotangent=cotangent, local_weight=local_weight, packed_codes=packed_codes, code_scales=code_scales, global_weight=global_weight, momentum=momentum)


epsilon = 1e-05
outer_rate = 0.7
outer_push = 0.9
keep_share = 0.5
inner_rate = 0.5

def decode(words, scales):
    planes = [jnp.bitwise_and(jnp.right_shift(words, 4 * plane), 15) - 8 for plane in range(2)]
    codes = jnp.concatenate(planes, axis=-1).astype(jnp.float32)
    layout = codes.shape
    grouped = codes.reshape(layout[:-1] + (layout[-1] // 128, 128)) * scales[..., None]
    return grouped.reshape(layout)

def reference(tokens_in, gain, cotangent, local_weight, packed_codes, code_scales, global_weight, momentum):
    factor = 1.0 / D ** 0.5

    def add_replica(carry, pair):
        return (carry + decode(pair[0], pair[1]), None)
    summed, unused = lax.scan(add_replica, jnp.zeros((D, KV_COLS), jnp.float32), (packed_codes, code_scales))
    delta = summed / N_REP
    glob = global_weight.reshape(D, KV_COLS)
    mom = momentum.reshape(D, KV_COLS)
    new_momentum = outer_push * mom + delta
    new_global = glob - outer_rate * (delta + outer_push * new_momentum)
    shared = lax.optimization_barrier(new_global.astype(jnp.bfloat16)).astype(jnp.float32)

    def replica(items):
        rows_in, cot_rows, weight = items
        wide = rows_in.astype(jnp.float32)
        mean_square = lax.optimization_barrier(jnp.mean(wide * wide, axis=-1, keepdims=True))
        inverse = lax.rsqrt(mean_square + epsilon)
        normed = (wide * inverse * gain).astype(jnp.bfloat16)
        total = jnp.zeros((TOK, KV_COLS), jnp.float32)
        for block in range(N_TP):
            lower = block * D_DEV
            partial_value = jnp.dot(normed[:, lower:lower + D_DEV], weight[lower:lower + D_DEV], preferred_element_type=jnp.float32) * factor
            total = total + lax.optimization_barrier(partial_value.astype(jnp.bfloat16)).astype(jnp.float32)
        projected = total.astype(jnp.bfloat16)
        grad_weight = lax.dot_general(normed, cot_rows, (((0,), (0,)), ((), ())), preferred_element_type=jnp.float32) * factor
        grad_normed = lax.dot_general(cot_rows, weight, (((1,), (1,)), ((), ())), preferred_element_type=jnp.float32) * factor
        scaled = gain * grad_normed
        inner = lax.optimization_barrier(jnp.sum(scaled * wide, axis=-1, keepdims=True))
        grad_x = (inverse * scaled - wide * inverse ** 3 * inner / D).astype(jnp.bfloat16)
        mixed = (keep_share * weight.astype(jnp.float32) + (1.0 - keep_share) * shared - inner_rate * grad_weight).astype(jnp.bfloat16)
        return (projected, grad_x, mixed)
    projected, grad_x, new_local = lax.map(replica, (tokens_in.reshape(N_REP, TOK, D), cotangent.reshape(N_REP, TOK, KV_COLS), local_weight))
    return (projected.reshape(TOKENS, KV_COLS), grad_x.reshape(TOKENS, D), new_local, new_global.reshape(N_TP, D_DEV, KV_COLS), new_momentum.reshape(N_TP, D_DEV, KV_COLS))
```

```python
import math

import jax
import jax.numpy as jnp
from jax import lax
from jax.experimental import pallas as pl
from jax.experimental.pallas import tpu as pltpu
from jax.sharding import PartitionSpec as P

MESH = pl.DeviceIdType.MESH
BF = jnp.bfloat16
F32 = jnp.float32

D = 8192
T = 1024
F = 1024
C = 1024
H = 512
L = 128
FACTOR = 1.0 / math.sqrt(D)

epsilon = 1e-05
outer_rate = 0.7
outer_push = 0.9
keep_share = 0.5
inner_rate = 0.5

SEMS = 96


def row_of(ref):
    return jnp.concatenate([ref[pl.ds(i, 1), :] for i in range(8)], axis=1)


def store_row(ref, row):
    for i in range(8):
        ref[pl.ds(i, 1), :] = row[:, i * L:(i + 1) * L]


def to_row(column_sums):
    return jnp.sum(jnp.transpose(column_sums), axis=0, keepdims=True)


def to_column(row):
    return jnp.transpose(jnp.broadcast_to(row, (L, T)))


def kernel(
    x_hbm, gain_hbm, cot_hbm, w_hbm, codes_hbm, scales_hbm, glob_hbm, mom_hbm,
    proj_hbm, gx_hbm, nl_hbm, ng_hbm, nm_hbm,
    x_v, gain_v, w_v, codes_v, scales_v, glob_v, mom_v,
    xg, xgt, cotf, csf, pf, pn, pown, ar, br, cr, zsend, zrecv,
    cores, corer, xs, xr, zs, zr, zown, sh,
    acc, invb, coefb, sqs, sqr, sqz, sqzr, ins, inr, inz, inzr,
    gn, gw, gx, nl, proj, ng, nm,
    send_sem, recv_sem, load_sem, out_sem,
):
    rep = lax.axis_index("rep")
    tp = lax.axis_index("tp")
    zl = rep // 8
    xx = (rep // 2) % 4
    c = rep % 2
    zh = tp // 4
    y = tp % 4

    def at_y(d):
        return (rep, zh * 4 + (y + d) % 4)

    def at_x(d):
        return (zl * 8 + ((xx + d) % 4) * 2 + c, tp)

    def at_z(d):
        return (((zl + d) % 4) * 8 + xx * 2 + c, tp)

    at_zh = (rep, (1 - zh) * 4 + y)
    at_core = (zl * 8 + xx * 2 + (1 - c), tp)

    counter = [0]

    def remote(src, dst, dev, landing=None):
        i = counter[0]
        counter[0] += 1
        send = pltpu.make_async_remote_copy(
            src_ref=src, dst_ref=dst, send_sem=send_sem.at[i], recv_sem=recv_sem.at[i],
            device_id=dev, device_id_type=MESH,
        )
        if landing is None:
            return send, send
        recv = pltpu.make_async_remote_copy(
            src_ref=src, dst_ref=landing, send_sem=send_sem.at[i], recv_sem=recv_sem.at[i],
            device_id=dev, device_id_type=MESH,
        )
        return send, recv

    sent = []

    def go(pair):
        pair[0].start()
        sent.append(pair[0])

    loads = {}
    for i, (name, src, dst) in enumerate((
        ("codes", codes_hbm, codes_v), ("scales", scales_hbm, scales_v),
        ("cot", cot_hbm, cotf.at[tp]), ("x", x_hbm, x_v), ("gain", gain_hbm, gain_v),
        ("w", w_hbm, w_v), ("glob", glob_hbm, glob_v), ("mom", mom_hbm, mom_v),
    )):
        loads[name] = pltpu.make_async_copy(src, dst, load_sem.at[i])
        loads[name].start()

    barrier = pltpu.get_barrier_semaphore()
    peers = [at_y(1), at_y(2), at_y(3), at_zh, at_core]
    peers += [at_x(d) for d in (1, 2, 3)] + [at_z(d) for d in (1, 2, 3)]
    for dev in peers:
        pl.semaphore_signal(barrier, inc=1, device_id=dev, device_id_type=MESH)

    def decoded(block, k):
        rows = pl.ds(pl.multiple_of(block * 32, 32), 32)
        words = codes_v[rows, :]
        codes = (jnp.bitwise_and(jnp.right_shift(words, 4 * k), 15) - 8).astype(F32)
        scales = scales_v[rows, :]
        return jnp.concatenate(
            [codes[:, g * L:(g + 1) * L] * scales[:, 4 * k + g:4 * k + g + 1] for g in range(4)], axis=1
        )

    loads["codes"].wait()
    loads["scales"].wait()
    offsets = (2, 1, 3, 0)

    for k in range(2):
        def for_partner(i, carry, k=k):
            cores[k, i // 4, i % 4] = decoded((i % 4) * 8 + (i // 4) * 2 + (1 - c), k).astype(BF)
            return carry
        lax.fori_loop(0, 16, for_partner, 0)

    loads["cot"].wait()
    pl.semaphore_wait(barrier, len(peers))

    other = (1 - zh) * 4 + y

    def block_of(half, d):
        return half * 4 + (y + d) % 4

    cot_z = remote(cotf.at[tp], cotf.at[tp], at_zh, cotf.at[other])
    cot_near = [
        remote(cotf.at[tp], cotf.at[tp], at_y(1), cotf.at[block_of(zh, 3)]),
        remote(cotf.at[tp], cotf.at[tp], at_y(3), cotf.at[block_of(zh, 1)]),
    ]
    go(cot_z)
    go(cot_near[0])
    go(cot_near[1])

    core_copies = {}
    for k in range(2):
        for d in offsets:
            xi = (xx + d) % 4
            core_copies[k, d] = remote(cores.at[k, xi], corer.at[k, xi], at_core)
            go(core_copies[k, d])

    loads["gain"].wait()
    loads["x"].wait()
    gain = gain_v[...]

    def scale_rows(i, carry):
        rows = pl.ds(pl.multiple_of(i * 32, 32), 32)
        wide = x_v[rows, :].astype(F32)
        xg[rows, :] = (wide * gain).astype(BF)
        squares = wide * wide
        total = squares[:, 0:L]
        for j in range(1, 8):
            total = total + squares[:, j * L:(j + 1) * L]
        acc[rows, :] = total
        return carry
    lax.fori_loop(0, 32, scale_rows, 0)
    loads["w"].wait()

    halves = (pl.ds(0, H), pl.ds(H, H))

    def weights(target):
        first = pl.ds(pl.multiple_of(((1 - zh) * 4 + target) * L, L), L)
        second = pl.ds(pl.multiple_of((zh * 4 + target) * L, L), L)
        return jnp.concatenate([w_v[:, first], w_v[:, second]], axis=1)

    def project(rows, cols):
        return jnp.dot(xg[rows, :], cols, preferred_element_type=F32)

    cols = weights((y + 2) % 4)
    far = {}
    for d in range(2):
        value = project(halves[d], cols)
        for q in range(2):
            pf[q, halves[d], :] = value[:, q * L:(q + 1) * L].astype(BF)
        for q in range(2):
            far[d, q] = remote(pf.at[q, halves[d]], ar.at[d, q], at_y((1, 3)[d]))
            go(far[d, q])

    store_row(sqs, to_row(acc[...]))
    sq_y = [remote(sqs, sqr.at[d - 1], at_y(d)) for d in (1, 2, 3)]
    for pair in sq_y:
        go(pair)

    x_copies = {}
    for k in range(2):
        for d in offsets:
            xi = (xx + d) % 4
            core_copies[k, d][1].wait_recv()

            def add_partner(zi, carry, k=k, xi=xi):
                both = decoded(zi * 8 + xi * 2 + c, k) + corer[k, xi, zi].astype(F32)
                xs[k, xi, zi] = both.astype(BF)
                return carry
            lax.fori_loop(0, 4, add_partner, 0)
            if d:
                x_copies[k, d] = remote(xs.at[k, xi], xr.at[k, d - 1], at_x(d))
                go(x_copies[k, d])

    near = {}
    for d in range(2):
        cols = weights((y + (1, 3)[d]) % 4)
        for h in (1 - d, d):
            value = project(halves[h], cols)
            for q in range(2):
                pn[d, q, halves[h], :] = value[:, q * L:(q + 1) * L].astype(BF)
            if h == 1 - d:
                for q in range(2):
                    near[d, q] = remote(pn.at[d, q, halves[h]], cr.at[d, q], at_y((1, 3)[d]))
                    go(near[d, q])

    onward = {}
    for q in range(2):
        for d in range(2):
            far[d, q][1].wait_recv()
            pn[d, q, halves[d], :] = (
                pn[d, q, halves[d], :].astype(F32) + ar[d, q].astype(F32)
            ).astype(BF)
            onward[d, q] = remote(pn.at[d, q, halves[d]], br.at[d, q], at_y((1, 3)[d]))
            go(onward[d, q])

    cols = weights(y)
    for h in range(2):
        value = project(halves[h], cols)
        for q in range(2):
            pown[q, halves[h], :] = value[:, q * L:(q + 1) * L]

    for pair in sq_y:
        pair[1].wait_recv()
    sqz[...] = sqs[...] + sqr[0] + sqr[1] + sqr[2]
    sq_z = remote(sqz, sqzr, at_zh)
    go(sq_z)

    def along_x(k):
        for d in (1, 2, 3):
            x_copies[k, d][1].wait_recv()

        def add(zi, carry, k=k):
            total = xs[k, xx, zi].astype(F32)
            for s in range(3):
                total = total + xr[k, s, zi].astype(F32)
            zs[k, zi] = total.astype(BF)
            return carry
        lax.fori_loop(0, 4, add, 0)
        copies = []
        for d in (2, 1, 3):
            copies.append(remote(zs.at[k, (zl + d) % 4], zr.at[k, d - 1], at_z(d)))
            go(copies[-1])
        return copies

    def outer(k, copies):
        for pair in copies:
            pair[1].wait_recv()
        total = zs[k, zl].astype(F32)
        for s in range(3):
            total = total + zr[k, s].astype(F32)
        delta = total * (1.0 / 32.0)
        part = pl.ds(k * H, H)
        new_momentum = outer_push * mom_v[:, part] + delta
        new_global = glob_v[:, part] - outer_rate * (delta + outer_push * new_momentum)
        nm[:, part] = new_momentum
        ng[:, part] = new_global
        sh[k, c, xx, zl] = new_global.astype(BF)
        copies = []
        for d in (2, 1, 3):
            here = sh.at[k, c, xx, zl]
            copies.append(remote(here, here, at_z(d), sh.at[k, c, xx, (zl - d + 4) % 4]))
            go(copies[-1])
        return copies

    def spread_x(k, copies):
        for pair in copies:
            pair[1].wait_recv()
        here = sh.at[k, c, xx]
        copies = {}
        for d in (2, 1, 3):
            copies[d] = remote(here, here, at_x(d), sh.at[k, c, (xx - d + 4) % 4])
            go(copies[d])
        copies[0] = remote(here, here, at_core, sh.at[k, 1 - c, xx])
        go(copies[0])
        return copies

    def spread_core(k, copies):
        arrivals = [copies[0]]
        for d in (1, 3, 2):
            copies[d][1].wait_recv()
            xi = (xx - d + 4) % 4
            here = sh.at[k, c, xi]
            arrivals.append(remote(here, here, at_core, sh.at[k, 1 - c, xi]))
            go(arrivals[-1])
        return arrivals

    z0 = along_x(0)

    cot_far = []
    for d in range(2):
        cot_near[d][1].wait_recv()
        came = block_of(zh, (3, 1)[d])
        part = cotf.at[came, halves[d]]
        cot_far.append(remote(part, part, at_y((1, 3)[d]), cotf.at[block_of(zh, 2), halves[d]]))
        go(cot_far[-1])
    cot_z[1].wait_recv()
    other_near = []
    for d in range(2):
        here = cotf.at[other]
        other_near.append(remote(here, here, at_y((1, 3)[d]), cotf.at[block_of(1 - zh, (3, 1)[d])]))
        go(other_near[-1])

    for j in range(4):
        xgt[pl.ds(j * 256, 256), :] = jnp.transpose(xg[:, pl.ds(j * 256, 256)])

    loads["glob"].wait()
    loads["mom"].wait()
    z1 = along_x(1)
    z0 = outer(0, z0)

    for h in range(2):
        onward[h, 0][1].wait_recv()
        near[1 - h, 0][1].wait_recv()
        total = pown[0, halves[h], :] + br[h, 0].astype(F32) + cr[1 - h, 0].astype(F32)
        zsend[halves[h], :] = total.astype(BF)
        acc[halves[h], :] = total * cotf[other, halves[h], :].astype(F32)
    proj_z = remote(zsend, zrecv, at_zh)
    go(proj_z)

    z1 = outer(1, z1)
    x0 = spread_x(0, z0)

    for h in range(2):
        onward[h, 1][1].wait_recv()
        near[1 - h, 1][1].wait_recv()
        total = pown[1, halves[h], :] + br[h, 1].astype(F32) + cr[1 - h, 1].astype(F32)
        pown[1, halves[h], :] = total
        acc[halves[h], :] = acc[halves[h], :] + total * cotf[tp, halves[h], :].astype(F32)
    store_row(ins, to_row(acc[...]))
    in_y = [remote(ins, inr.at[d - 1], at_y(d)) for d in (1, 2, 3)]
    for pair in in_y:
        go(pair)

    x1 = spread_x(1, z1)

    sq_z[1].wait_recv()
    squares = row_of(sqz) + row_of(sqzr)
    inverse = lax.rsqrt(squares * (1.0 / D) + epsilon)
    invb[...] = to_column(inverse)

    for pair in cot_far:
        pair[1].wait_recv()

    def group(half, first):
        for j in range(4):
            csf[half * 4 + j] = (cotf[half * 4 + j].astype(F32) * invb[...]).astype(BF)

        def weight_part(j, carry):
            right = jnp.concatenate([csf[half * 4 + 2 * j], csf[half * 4 + 2 * j + 1]], axis=1)
            part = pl.ds(pl.multiple_of(j * 256, 256), 256)
            gw[half, :, part] = jnp.dot(xgt[...], right, preferred_element_type=F32)
            return carry
        lax.fori_loop(0, 2, weight_part, 0)

    def normed_part(half, j):
        left = jnp.concatenate([cotf[half * 4 + i] for i in range(4)], axis=1)
        rows = pl.ds(pl.multiple_of(j * 256, 256), 256)
        right = w_v[rows, pl.ds(pl.multiple_of(half * H, H), H)]
        return lax.dot_general(left, right, (((1,), (1,)), ((), ())), preferred_element_type=F32)

    def keep_part(j, carry):
        gn[j] = normed_part(zh, j)
        return carry
    lax.fori_loop(0, 4, keep_part, 0)
    group(zh, True)

    for pair in in_y:
        pair[1].wait_recv()
    inz[...] = ins[...] + inr[0] + inr[1] + inr[2]
    in_z = remote(inz, inzr, at_zh)
    go(in_z)

    other_far = []
    for d in range(2):
        other_near[d][1].wait_recv()
        came = block_of(1 - zh, (3, 1)[d])
        part = cotf.at[came, halves[d]]
        other_far.append(remote(part, part, at_y((1, 3)[d]), cotf.at[block_of(1 - zh, 2), halves[d]]))
        go(other_far[-1])

    c0 = spread_core(0, x0)

    proj_z[1].wait_recv()
    proj[...] = ((pown[1] + zrecv[...].astype(F32)) * invb[...] * FACTOR).astype(BF)
    outs = [
        pltpu.make_async_copy(proj, proj_hbm, out_sem.at[0]),
        pltpu.make_async_copy(ng, ng_hbm, out_sem.at[1]),
        pltpu.make_async_copy(nm, nm_hbm, out_sem.at[2]),
    ]
    for copy in outs:
        copy.start()

    c1 = spread_core(1, x1)

    in_z[1].wait_recv()
    inner = row_of(inz) + row_of(inzr)
    coefb[...] = to_column(inverse * inverse * inverse * inner * (FACTOR / D))
    for pair in other_far:
        pair[1].wait_recv()

    def finish_x(j, carry):
        part = pl.ds(pl.multiple_of(j * 256, 256), 256)
        value = (gn[j] + normed_part(1 - zh, j)) * (gain_v[:, part] * FACTOR)
        scale = jnp.concatenate([invb[...]] * 2, axis=1)
        coef = jnp.concatenate([coefb[...]] * 2, axis=1)
        gx[:, part] = (value * scale - x_v[:, part].astype(F32) * coef).astype(BF)
        copy = pltpu.make_async_copy(gx.at[:, part], gx_hbm.at[:, part], out_sem.at[4 + j])
        copy.start()
        return carry
    lax.fori_loop(0, 4, finish_x, 0)

    group(1 - zh, False)
    for k, arrivals in ((0, c0), (1, c1)):
        for pair in arrivals:
            pair[1].wait_recv()

    def finish_w(b, carry):
        rows = pl.ds(pl.multiple_of(b * 32, 32), 32)
        for k in range(2):
            part = pl.ds(k * H, H)
            mixed = (
                keep_share * w_v[rows, part].astype(F32)
                + (1.0 - keep_share) * sh[k, b % 2, (b // 2) % 4, b // 8].astype(F32)
                - (inner_rate * FACTOR) * gw[k, rows, :]
            )
            nl[rows, part] = mixed.astype(BF)
        return carry

    for q in range(4):
        lax.fori_loop(8 * q, 8 * q + 8, finish_w, 0)
        rows = pl.ds(q * 256, 256)
        copy = pltpu.make_async_copy(nl.at[rows], nl_hbm.at[rows], out_sem.at[8 + q])
        copy.start()
        outs.append(copy)
    for j in range(4):
        part = pl.ds(j * 256, 256)
        outs.append(pltpu.make_async_copy(gx.at[:, part], gx_hbm.at[:, part], out_sem.at[4 + j]))
    for copy in outs:
        copy.wait()
    for copy in sent:
        copy.wait_send()
    assert counter[0] <= SEMS


def local(
    tokens_in, gain, cotangent, local_weight, packed_codes, code_scales, global_weight, momentum
):
    any_ = pl.BlockSpec(memory_space=pl.ANY)
    vm = pltpu.VMEM
    projected, grad_x, new_local, new_global, new_momentum = pl.pallas_call(
        kernel,
        out_shape=(
            jax.ShapeDtypeStruct((T, L), BF),
            jax.ShapeDtypeStruct((T, F), BF),
            jax.ShapeDtypeStruct((F, C), BF),
            jax.ShapeDtypeStruct((32, C), F32),
            jax.ShapeDtypeStruct((32, C), F32),
        ),
        in_specs=[any_] * 8,
        out_specs=[any_] * 5,
        scratch_shapes=[
            vm((T, F), BF), vm((1, F), F32), vm((F, C), BF), vm((F, C // 2), jnp.int32), vm((F, 8), F32),
            vm((32, C), F32), vm((32, C), F32),
            vm((T, F), BF), vm((F, T), BF), vm((8, T, L), BF), vm((8, T, L), BF),
            vm((2, T, L), BF), vm((2, 2, T, L), BF), vm((2, T, L), F32),
            vm((2, 2, H, L), BF), vm((2, 2, H, L), BF), vm((2, 2, H, L), BF),
            vm((T, L), BF), vm((T, L), BF),
            vm((2, 4, 4, 32, H), BF), vm((2, 4, 4, 32, H), BF), vm((2, 4, 4, 32, H), BF),
            vm((2, 3, 4, 32, H), BF), vm((2, 4, 32, H), BF), vm((2, 3, 32, H), BF), vm((8, L), F32),
            vm((2, 2, 4, 4, 32, H), BF),
            vm((T, L), F32), vm((T, L), F32), vm((T, L), F32),
            vm((8, L), F32), vm((3, 8, L), F32), vm((8, L), F32), vm((8, L), F32),
            vm((8, L), F32), vm((3, 8, L), F32), vm((8, L), F32), vm((8, L), F32),
            vm((4, T, 256), F32), vm((2, F, H), F32), vm((T, F), BF), vm((F, C), BF),
            vm((T, L), BF), vm((32, C), F32), vm((32, C), F32),
            pltpu.SemaphoreType.DMA((SEMS,)), pltpu.SemaphoreType.DMA((SEMS,)),
            pltpu.SemaphoreType.DMA((8,)), pltpu.SemaphoreType.DMA((12,)),
        ],
        compiler_params=pltpu.CompilerParams(
            collective_id=0, has_side_effects=True, vmem_limit_bytes=60 * 2**20
        ),
        cost_estimate=pl.CostEstimate(flops=6 * 2**30, bytes_accessed=12 * 2**20, transcendentals=0),
    )(
        tokens_in, gain.reshape(1, F), cotangent, local_weight[0], packed_codes[0], code_scales[0],
        global_weight[0], momentum[0],
    )
    return (projected, grad_x, new_local[None], new_global[None], new_momentum[None])


def solution(mesh):
    return jax.shard_map(
        local,
        mesh=mesh,
        in_specs=(
            P("rep", "tp"),
            P("tp"),
            P("rep", "tp"),
            P("rep", "tp", None),
            P("rep", "tp", None),
            P("rep", "tp", None),
            P("tp", "rep", None),
            P("tp", "rep", None),
        ),
        out_specs=(
            P("rep", "tp"),
            P("rep", "tp"),
            P("rep", "tp", None),
            P("tp", "rep", None),
            P("tp", "rep", None),
        ),
        check_vma=False,
    )
```

```python
import math

import jax
import jax.numpy as jnp
from jax import lax
from jax.experimental import pallas as pl
from jax.experimental.pallas import tpu as pltpu
from jax.sharding import PartitionSpec as P

MESH = pl.DeviceIdType.MESH
BF = jnp.bfloat16
F32 = jnp.float32

D = 8192
T = 1024
F = 1024
C = 1024
H = 512
L = 128
FACTOR = 1.0 / math.sqrt(D)

epsilon = 1e-05
outer_rate = 0.7
outer_push = 0.9
keep_share = 0.5
inner_rate = 0.5

SEMS = 48


def row_of(ref):
    return jnp.concatenate([ref[pl.ds(i, 1), :] for i in range(8)], axis=1)


def store_row(ref, row):
    for i in range(8):
        ref[pl.ds(i, 1), :] = row[:, i * L:(i + 1) * L]


def to_row(column_sums):
    return jnp.sum(jnp.transpose(column_sums), axis=0, keepdims=True)


def to_column(row):
    return jnp.transpose(jnp.broadcast_to(row, (L, T)))


def kernel(
    x_hbm, gain_hbm, cot_hbm, w_hbm, codes_hbm, scales_hbm, glob_hbm, mom_hbm,
    proj, gx, nl, ng, nm,
    x_v, gain_v, w_v, codes_v, scalest_v, scales_v, glob_v, mom_v,
    xg, xgt, cotf, csf, pf, pn, pown, ar, br, cr, zsend, zrecv,
    cores, corer, xs, xr, zs, zr, zown, sh,
    acc, invb, coefb, sqs, sqr, sqz, sqzr, ins, inr, inz, inzr,
    gn, gw,
    send_sem, recv_sem, load_sem,
):
    rep = lax.axis_index("rep")
    tp = lax.axis_index("tp")
    zl = rep // 8
    xx = (rep // 2) % 4
    c = rep % 2
    zh = tp // 4
    y = tp % 4

    def at_y(d):
        return (rep, zh * 4 + (y + d) % 4)

    def at_x(d):
        return (zl * 8 + ((xx + d) % 4) * 2 + c, tp)

    def at_z(d):
        return (((zl + d) % 4) * 8 + xx * 2 + c, tp)

    at_zh = (rep, (1 - zh) * 4 + y)
    at_core = (zl * 8 + xx * 2 + (1 - c), tp)

    slots = {"send": {}, "recv": {}}

    def slot(kind, key):
        return slots[kind].setdefault(key, len(slots[kind]))

    def describe(src, dst, dev, send_key, recv_key):
        return pltpu.make_async_remote_copy(
            src_ref=src, dst_ref=dst,
            send_sem=send_sem.at[slot("send", send_key)], recv_sem=recv_sem.at[slot("recv", recv_key)],
            device_id=dev, device_id_type=MESH,
        )

    def go(src, dst, dev, send_key, recv_key):
        describe(src, dst, dev, send_key, recv_key).start()

    def arrived(recv_key, like):
        describe(like, like, at_core, "none", recv_key).wait_recv()

    def departed(send_key, like):
        describe(like, like, at_core, send_key, "none").wait_send()

    loads = {}
    for i, (name, src, dst) in enumerate((
        ("scales", scales_hbm, scalest_v), ("codes", codes_hbm, codes_v),
        ("cot", cot_hbm, cotf.at[tp]), ("gain", gain_hbm, gain_v), ("x", x_hbm, x_v),
        ("w", w_hbm, w_v), ("glob", glob_hbm, glob_v), ("mom", mom_hbm, mom_v),
    )):
        loads[name] = pltpu.make_async_copy(src, dst, load_sem.at[i])
        loads[name].start()

    barrier = pltpu.get_barrier_semaphore()
    peers = [at_y(1), at_y(2), at_y(3), at_zh, at_core]
    peers += [at_x(d) for d in (1, 2, 3)] + [at_z(d) for d in (1, 2, 3)]
    for dev in peers:
        pl.semaphore_signal(barrier, inc=1, device_id=dev, device_id_type=MESH)

    def half_of(k):
        return zh if k == 0 else 1 - zh

    def columns_of(k):
        return pl.ds(pl.multiple_of(half_of(k) * H, H), H)

    def decoded(block, k):
        rows = pl.ds(pl.multiple_of(block * 32, 32), 32)
        words = codes_v[rows, :]
        codes = (jnp.bitwise_and(jnp.right_shift(words, 4 * half_of(k)), 15) - 8).astype(F32)
        scales = scales_v[k, rows, :]
        return jnp.concatenate(
            [codes[:, g * L:(g + 1) * L] * scales[:, g:g + 1] for g in range(4)], axis=1
        )

    offsets = (2, 1, 3, 0)
    near_dev = (at_y(1), at_y(3))
    halves = (pl.ds(0, H), pl.ds(H, H))
    other = (1 - zh) * 4 + y

    def block_of(half, d):
        return half * 4 + (y + d) % 4

    loads["scales"].wait()
    all_scales = jnp.transpose(scalest_v[...])
    first, second = all_scales[:, 0:4], all_scales[:, 4:8]
    scales_v[0] = jnp.where(zh == 0, first, second)
    scales_v[1] = jnp.where(zh == 0, second, first)
    loads["codes"].wait()
    for k in range(2):
        def for_partner(i, carry, k=k):
            cores[k, i // 4, i % 4] = decoded((i % 4) * 8 + (i // 4) * 2 + (1 - c), k).astype(BF)
            return carry
        lax.fori_loop(0, 16, for_partner, 0, unroll=4)

    loads["gain"].wait()
    loads["x"].wait()
    gain = gain_v[...]

    def scale_rows(i, carry):
        rows = pl.ds(pl.multiple_of(i * 32, 32), 32)
        wide = x_v[rows, :].astype(F32)
        xg[rows, :] = (wide * gain).astype(BF)
        squares = wide * wide
        total = squares[:, 0:L]
        for j in range(1, 8):
            total = total + squares[:, j * L:(j + 1) * L]
        acc[rows, :] = total
        return carry
    lax.fori_loop(0, 32, scale_rows, 0, unroll=4)

    loads["cot"].wait()
    pl.semaphore_wait(barrier, len(peers))

    for k in range(2):
        go(cores.at[k], corer.at[k], at_core, "core", ("core", k))

    def to_other(first, rows):
        mine = cotf.at[tp, pl.ds(first, rows)]
        go(mine, mine, at_zh, "cot", "cot_z")

    to_other(0, 1024)

    def to_near(half, h, d, key):
        mine = cotf.at[half * 4 + y, halves[h]]
        go(mine, mine, near_dev[d], "cot", key)

    def to_far(half, d, key):
        part = cotf.at[block_of(half, (3, 1)[d]), halves[d]]
        go(part, part, near_dev[d], "cot", key)

    for d in range(2):
        to_near(zh, d, d, "first")
    store_row(sqs, to_row(acc[...]))
    for d in (1, 2, 3):
        go(sqs, sqr.at[d - 1], at_y(d), "sq_y", "sq_y")
    loads["w"].wait()

    def weights(target):
        first = pl.ds(pl.multiple_of(((1 - zh) * 4 + target) * L, L), L)
        second = pl.ds(pl.multiple_of((zh * 4 + target) * L, L), L)
        return jnp.concatenate([w_v[:, first], w_v[:, second]], axis=1)

    def project(rows, cols):
        return jnp.dot(xg[rows, :], cols, preferred_element_type=F32)

    def send_far(d, q):
        go(pf.at[q, halves[d]], ar.at[d, q], near_dev[d], "proj", ("far", q))

    def send_near(d, q):
        go(pn.at[d, q, halves[1 - d]], cr.at[d, q], near_dev[d], "proj", ("near", q))

    def send_onward(q):
        arrived(("far", q), pf.at[q])
        for d in range(2):
            pn[d, q, halves[d], :] = (
                pn[d, q, halves[d], :].astype(F32) + ar[d, q].astype(F32)
            ).astype(BF)
            go(pn.at[d, q, halves[d]], br.at[d, q], near_dev[d], "proj", ("near", q))

    def add_own(k):
        arrived(("core", k), corer.at[k])
        for d in offsets:
            xi = (xx + d) % 4

            def add_partner(zi, carry, k=k, xi=xi):
                both = decoded(zi * 8 + xi * 2 + c, k) + corer[k, xi, zi].astype(F32)
                xs[k, xi, zi] = both.astype(BF)
                return carry
            lax.fori_loop(0, 4, add_partner, 0, unroll=4)
            if d:
                go(xs.at[k, xi], xr.at[k, d - 1], at_x(d), "x", ("x", k))

    cols = weights((y + 2) % 4)
    for d in range(2):
        value = project(halves[d], cols)
        for q in range(2):
            pf[q, halves[d], :] = value[:, q * L:(q + 1) * L].astype(BF)
        send_far(d, 0)
    add_own(0)
    for d in range(2):
        cols = weights((y + (1, 3)[d]) % 4)
        for h in (1 - d, d):
            value = project(halves[h], cols)
            for q in range(2):
                pn[d, q, halves[h], :] = value[:, q * L:(q + 1) * L].astype(BF)
            if h == 1 - d:
                send_near(d, 0)
    add_own(1)

    cols = weights(y)
    for h in range(2):
        value = project(halves[h], cols)
        for q in range(2):
            pown[q, halves[h], :] = value[:, q * L:(q + 1) * L]

    send_onward(0)
    for d in range(2):
        send_far(d, 1)
    for d in range(2):
        send_near(d, 1)

    arrived("sq_y", sqr)
    sqz[...] = sqs[...] + sqr[0] + sqr[1] + sqr[2]
    go(sqz, sqzr, at_zh, "sq_z", "sq_z")

    def along_x(k):
        arrived(("x", k), xr.at[k])

        def add(zi, carry, k=k):
            total = xs[k, xx, zi].astype(F32)
            for s in range(3):
                total = total + xr[k, s, zi].astype(F32)
            zs[k, zi] = total.astype(BF)
            return carry
        lax.fori_loop(0, 4, add, 0, unroll=4)
        for d in (2, 1, 3):
            go(zs.at[k, (zl + d) % 4], zr.at[k, d - 1], at_z(d), "z", ("z", k))

    def outer(k):
        arrived(("z", k), zr.at[k])
        total = zs[k, zl].astype(F32)
        for s in range(3):
            total = total + zr[k, s].astype(F32)
        delta = total * (1.0 / 32.0)
        part = columns_of(k)
        new_momentum = outer_push * mom_v[:, part] + delta
        new_global = glob_v[:, part] - outer_rate * (delta + outer_push * new_momentum)
        nm[:, part] = new_momentum
        ng[:, part] = new_global
        sh[k, c, xx, zl] = new_global.astype(BF)
        here = sh.at[k, c, xx, zl]
        for d in (2, 1, 3):
            go(here, here, at_z(d), "z_back", ("z_back", k))

    def spread_x(k):
        arrived(("z_back", k), zr.at[k])
        here = sh.at[k, c, xx]
        for d in (2, 1, 3):
            go(here, here, at_x(d), "x_back", ("x_back", k))

    def spread_core(k):
        arrived(("x_back", k), xr.at[k])
        go(sh.at[k, c], sh.at[k, c], at_core, "core_back", ("core_back", k))

    def transpose_part(j):
        xgt[pl.ds(j * 256, 256), :] = jnp.transpose(xg[:, pl.ds(j * 256, 256)])

    def send_proj(first, rows):
        part = zsend.at[pl.ds(first, rows)]
        go(part, zrecv.at[pl.ds(first, rows)], at_zh, "proj_z", "proj_z")

    def gather_part(q):
        arrived(("near", q), pf)
        for h in range(2):
            total = pown[q, halves[h], :] + br[h, q].astype(F32) + cr[1 - h, q].astype(F32)
            pown[q, halves[h], :] = total
            if q == 0:
                zsend[halves[h], :] = total.astype(BF)

    def weight_grad(blocks):
        for block in blocks:
            csf[block] = (cotf[block].astype(F32) * invb[...]).astype(BF)
        for i in range(0, len(blocks), 2):
            some = blocks[i:i + 2]
            right = jnp.concatenate([csf[block] for block in some], axis=1)
            value = jnp.dot(xgt[...], right, preferred_element_type=F32)
            for at, block in enumerate(some):
                gw[block] = value[:, at * L:(at + 1) * L]

    def normed_part(blocks, j):
        left = jnp.concatenate([cotf[block] for block in blocks], axis=1)
        rows = pl.ds(pl.multiple_of(j * 256, 256), 256)
        right = jnp.concatenate(
            [w_v[rows, pl.ds(pl.multiple_of(block * L, L), L)] for block in blocks], axis=1
        )
        return lax.dot_general(left, right, (((1,), (1,)), ((), ())), preferred_element_type=F32)

    def normed_grad(blocks, add):
        def keep_part(j, carry):
            value = normed_part(blocks, j)
            gn[j] = gn[j] + value if add else value
            return carry
        lax.fori_loop(0, 4, keep_part, 0)

    def finish_w(k):
        half = half_of(k)

        def block(b, carry):
            rows = pl.ds(pl.multiple_of(b * 32, 32), 32)
            part = columns_of(k)
            step = jnp.concatenate([gw[half * 4 + j, rows, :] for j in range(4)], axis=1)
            mixed = (
                keep_share * w_v[rows, part].astype(F32)
                + (1.0 - keep_share) * sh[k, b % 2, (b // 2) % 4, b // 8].astype(F32)
                - (inner_rate * FACTOR) * step
            )
            nl[rows, part] = mixed.astype(BF)
            return carry
        lax.fori_loop(0, 32, block, 0, unroll=4)

    for j in range(4):
        transpose_part(j)
    normed_grad([tp], False)
    along_x(0)

    gather_part(0)
    send_proj(64, 64)

    send_onward(1)
    for d in range(2):
        to_near(zh, 1 - d, d, "rest")

    along_x(1)
    loads["glob"].wait()
    loads["mom"].wait()
    outer(0)
    send_proj(0, 64)

    arrived("sq_z", sqzr)
    squares = row_of(sqz) + row_of(sqzr)
    inverse = lax.rsqrt(squares * (1.0 / D) + epsilon)
    invb[...] = to_column(inverse)
    arrived("cot_z", cotf.at[other])
    acc[...] = pown[0] * cotf[other].astype(F32)
    weight_grad([tp, other])

    outer(1)
    send_proj(128, 256)

    gather_part(1)
    acc[...] = acc[...] + pown[1] * cotf[tp].astype(F32)
    store_row(ins, to_row(acc[...]))
    for d in (1, 2, 3):
        go(ins, inr.at[d - 1], at_y(d), "in_y", "in_y")

    arrived("first", cotf.at[0])
    for d in range(2):
        to_far(zh, d, "rest")
    for d in range(2):
        to_near(1 - zh, d, d, "other_first")
    for d in range(2):
        to_near(1 - zh, 1 - d, d, "other_rest")

    spread_x(0)

    arrived("in_y", inr)
    inz[...] = ins[...] + inr[0] + inr[1] + inr[2]
    go(inz, inzr, at_zh, "in_z", "in_z")
    send_proj(384, 640)

    spread_x(1)

    arrived("rest", cotf.at[pl.ds(0, 2)])
    near_blocks = [block_of(zh, d) for d in (1, 3)]
    normed_grad([other] + near_blocks + [block_of(zh, 2)], True)

    arrived("other_first", cotf.at[0])
    for d in range(2):
        to_far(1 - zh, d, "other_rest")

    weight_grad(near_blocks)
    spread_core(0)

    arrived("in_z", inzr)
    inner = row_of(inz) + row_of(inzr)
    coefb[...] = to_column(inverse * inverse * inverse * inner * (FACTOR / D))
    arrived("other_rest", cotf.at[pl.ds(0, 2)])
    near_blocks = [block_of(1 - zh, d) for d in (1, 3)]
    last = near_blocks + [block_of(1 - zh, 2)]

    def finish_x(j, carry):
        part = pl.ds(pl.multiple_of(j * 256, 256), 256)
        value = (gn[j] + normed_part(last, j)) * (gain_v[:, part] * FACTOR)
        scale = jnp.concatenate([invb[...]] * 2, axis=1)
        coef = jnp.concatenate([coefb[...]] * 2, axis=1)
        gx[:, part] = (value * scale - x_v[:, part].astype(F32) * coef).astype(BF)
        return carry
    lax.fori_loop(0, 4, finish_x, 0)

    weight_grad([block_of(zh, 2), block_of(1 - zh, 2)])
    weight_grad(near_blocks)
    spread_core(1)
    arrived("proj_z", zrecv)
    proj[...] = ((pown[1] + zrecv[...].astype(F32)) * invb[...] * FACTOR).astype(BF)
    arrived(("core_back", 0), corer.at[0])
    finish_w(0)
    arrived(("core_back", 1), corer.at[1])
    finish_w(1)

    departed("cot", cotf.at[pl.ds(0, 7)])
    departed("proj", cotf.at[pl.ds(0, 6)])
    departed("proj_z", zsend)
    departed("x", xr)
    departed("z", zr)
    departed("z_back", zr)
    departed("x_back", xr)
    departed("core", cores)
    departed("core_back", cores)
    departed("sq_y", sqr)
    departed("in_y", inr)
    departed("sq_z", sqz)
    departed("in_z", inz)
    assert max(len(used) for used in slots.values()) <= SEMS


def writer(*refs):
    sources, targets, sem = refs[:5], refs[5:10], refs[10]
    copies = [pltpu.make_async_copy(s, t, sem.at[i]) for i, (s, t) in enumerate(zip(sources, targets))]
    for copy in copies:
        copy.start()
    for copy in copies:
        copy.wait()


def local(
    tokens_in, gain, cotangent, local_weight, packed_codes, code_scales, global_weight, momentum
):
    any_ = pl.BlockSpec(memory_space=pltpu.HBM)
    vm = pltpu.VMEM
    shapes = (((T, L), BF), ((T, F), BF), ((F, C), BF), ((32, C), F32), ((32, C), F32))
    results = pl.pallas_call(
        kernel,
        out_shape=tuple(vm(*shape) for shape in shapes),
        in_specs=[any_] * 8,
        out_specs=[pl.BlockSpec(memory_space=vm)] * 5,
        scratch_shapes=[
            vm((T, F), BF), vm((1, F), F32), vm((F, C), BF), vm((F, C // 2), jnp.int32), vm((8, F), F32), vm((2, F, 4), F32),
            vm((32, C), F32), vm((32, C), F32),
            vm((T, F), BF), vm((F, T), BF), vm((8, T, L), BF), vm((8, T, L), BF),
            vm((2, T, L), BF), vm((2, 2, T, L), BF), vm((2, T, L), F32),
            vm((2, 2, H, L), BF), vm((2, 2, H, L), BF), vm((2, 2, H, L), BF),
            vm((T, L), BF), vm((T, L), BF),
            vm((2, 4, 4, 32, H), BF), vm((2, 4, 4, 32, H), BF), vm((2, 4, 4, 32, H), BF),
            vm((2, 3, 4, 32, H), BF), vm((2, 4, 32, H), BF), vm((2, 3, 32, H), BF), vm((8, L), F32),
            vm((2, 2, 4, 4, 32, H), BF),
            vm((T, L), F32), vm((T, L), F32), vm((T, L), F32),
            vm((8, L), F32), vm((3, 8, L), F32), vm((8, L), F32), vm((8, L), F32),
            vm((8, L), F32), vm((3, 8, L), F32), vm((8, L), F32), vm((8, L), F32),
            vm((4, T, 256), F32), vm((8, F, L), F32),
            pltpu.SemaphoreType.DMA((SEMS,)), pltpu.SemaphoreType.DMA((SEMS,)),
            pltpu.SemaphoreType.DMA((8,)),
        ],
        compiler_params=pltpu.CompilerParams(
            collective_id=0, has_side_effects=True, vmem_limit_bytes=48 * 2**20
        ),
        cost_estimate=pl.CostEstimate(flops=6 * 2**30, bytes_accessed=12 * 2**20, transcendentals=0),
    )(*(
        pltpu.with_memory_space_constraint(arg, pltpu.HBM) for arg in (
            tokens_in, gain.reshape(1, F), cotangent, local_weight[0], packed_codes[0], code_scales[0].T,
            global_weight[0], momentum[0],
        )
    ))
    projected, grad_x, new_local, new_global, new_momentum = pl.pallas_call(
        writer,
        out_shape=tuple(jax.ShapeDtypeStruct(*shape) for shape in shapes),
        in_specs=[pl.BlockSpec(memory_space=vm)] * 5,
        out_specs=[any_] * 5,
        scratch_shapes=[pltpu.SemaphoreType.DMA((5,))],
        compiler_params=pltpu.CompilerParams(vmem_limit_bytes=8 * 2**20),
    )(*results)
    return (projected, grad_x, new_local[None], new_global[None], new_momentum[None])


def solution(mesh):
    return jax.shard_map(
        local,
        mesh=mesh,
        in_specs=(
            P("rep", "tp"),
            P("tp"),
            P("rep", "tp"),
            P("rep", "tp", None),
            P("rep", "tp", None),
            P("rep", "tp", None),
            P("tp", "rep", None),
            P("tp", "rep", None),
        ),
        out_specs=(
            P("rep", "tp"),
            P("rep", "tp"),
            P("rep", "tp", None),
            P("tp", "rep", None),
            P("tp", "rep", None),
        ),
        check_vma=False,
    )
```

```python
import math

import jax
import jax.numpy as jnp
from jax import lax
from jax.experimental import pallas as pl
from jax.experimental.pallas import tpu as pltpu
from jax.sharding import PartitionSpec as P

MESH = pl.DeviceIdType.MESH
BF = jnp.bfloat16
F32 = jnp.float32

D = 8192
T = 1024
F = 1024
C = 1024
H = 512
Q = 256
PARTS = 4
L = 128
FACTOR = 1.0 / math.sqrt(D)

epsilon = 1e-05
outer_rate = 0.7
outer_push = 0.9
keep_share = 0.5
inner_rate = 0.5

SEMS = 48


def row_of(ref):
    return jnp.concatenate([ref[pl.ds(i, 1), :] for i in range(8)], axis=1)


def store_row(ref, row):
    for i in range(8):
        ref[pl.ds(i, 1), :] = row[:, i * L:(i + 1) * L]


def to_row(column_sums):
    return jnp.sum(jnp.transpose(column_sums), axis=0, keepdims=True)


def to_column(row):
    return jnp.transpose(jnp.broadcast_to(row, (L, T)))


def kernel(
    x_hbm, gain_hbm, cot_hbm, w_hbm, codes_hbm, scales_hbm, glob_hbm, mom_hbm,
    proj, gx, nl, ng, nm,
    x_v, gain_v, w_v, codes_v, scalest_v, scales_v, glob_v, mom_v,
    xg, xgt, cotf, csf, pf, pn, pown, ar, br, cr, zsend, zrecv,
    cores, corer, xs, xr, zs, zr, zown, sh,
    acc, invb, coefb, sqs, sqr, sqz, sqzr, ins, inr, inz, inzr,
    gn, gw,
    send_sem, recv_sem, load_sem,
):
    rep = lax.axis_index("rep")
    tp = lax.axis_index("tp")
    zl = rep // 8
    xx = (rep // 2) % 4
    c = rep % 2
    zh = tp // 4
    y = tp % 4

    def at_y(d):
        return (rep, zh * 4 + (y + d) % 4)

    def at_x(d):
        return (zl * 8 + ((xx + d) % 4) * 2 + c, tp)

    def at_z(d):
        return (((zl + d) % 4) * 8 + xx * 2 + c, tp)

    at_zh = (rep, (1 - zh) * 4 + y)
    at_core = (zl * 8 + xx * 2 + (1 - c), tp)

    slots = {"send": {}, "recv": {}}

    def slot(kind, key):
        return slots[kind].setdefault(key, len(slots[kind]))

    def describe(src, dst, dev, send_key, recv_key):
        return pltpu.make_async_remote_copy(
            src_ref=src, dst_ref=dst,
            send_sem=send_sem.at[slot("send", send_key)], recv_sem=recv_sem.at[slot("recv", recv_key)],
            device_id=dev, device_id_type=MESH,
        )

    def go(src, dst, dev, send_key, recv_key):
        describe(src, dst, dev, send_key, recv_key).start()

    def arrived(recv_key, like):
        describe(like, like, at_core, "none", recv_key).wait_recv()

    def departed(send_key, like):
        describe(like, like, at_core, send_key, "none").wait_send()

    loads = {}
    for i, (name, src, dst) in enumerate((
        ("scales", scales_hbm, scalest_v), ("codes", codes_hbm, codes_v),
        ("cot", cot_hbm, cotf.at[tp]), ("gain", gain_hbm, gain_v), ("x", x_hbm, x_v),
        ("w", w_hbm, w_v), ("glob", glob_hbm, glob_v), ("mom", mom_hbm, mom_v),
    )):
        loads[name] = pltpu.make_async_copy(src, dst, load_sem.at[i])
        loads[name].start()

    barrier = pltpu.get_barrier_semaphore()
    peers = [at_y(1), at_y(2), at_y(3), at_zh, at_core]
    peers += [at_x(d) for d in (1, 2, 3)] + [at_z(d) for d in (1, 2, 3)]
    for dev in peers:
        pl.semaphore_signal(barrier, inc=1, device_id=dev, device_id_type=MESH)

    def half_of(m):
        return zh if m == 0 else 1 - zh

    def columns_of(k):
        return pl.ds(pl.multiple_of(half_of(k // 2) * H + (k % 2) * Q, Q), Q)

    def decoded(block, k):
        rows = pl.ds(pl.multiple_of(block * 32, 32), 32)
        words = codes_v[rows, pl.ds((k % 2) * Q, Q)]
        codes = (jnp.bitwise_and(jnp.right_shift(words, 4 * half_of(k // 2)), 15) - 8).astype(F32)
        scales = scales_v[k // 2, rows, :]
        return jnp.concatenate(
            [codes[:, g * L:(g + 1) * L] * scales[:, (k % 2) * 2 + g:(k % 2) * 2 + g + 1] for g in range(2)],
            axis=1,
        )

    offsets = (2, 1, 3, 0)
    near_dev = (at_y(1), at_y(3))
    halves = (pl.ds(0, H), pl.ds(H, H))
    other = (1 - zh) * 4 + y

    def block_of(half, d):
        return half * 4 + (y + d) % 4

    loads["scales"].wait()
    all_scales = jnp.transpose(scalest_v[...])
    first, second = all_scales[:, 0:4], all_scales[:, 4:8]
    scales_v[0] = jnp.where(zh == 0, first, second)
    scales_v[1] = jnp.where(zh == 0, second, first)
    loads["codes"].wait()
    for k in range(PARTS):
        def for_partner(i, carry, k=k):
            cores[k, i // 4, i % 4] = decoded((i % 4) * 8 + (i // 4) * 2 + (1 - c), k).astype(BF)
            return carry
        lax.fori_loop(0, 16, for_partner, 0, unroll=4)

    loads["gain"].wait()
    loads["x"].wait()
    gain = gain_v[...]

    def scale_rows(i, carry):
        rows = pl.ds(pl.multiple_of(i * 32, 32), 32)
        wide = x_v[rows, :].astype(F32)
        xg[rows, :] = (wide * gain).astype(BF)
        squares = wide * wide
        total = squares[:, 0:L]
        for j in range(1, 8):
            total = total + squares[:, j * L:(j + 1) * L]
        acc[rows, :] = total
        return carry
    lax.fori_loop(0, 32, scale_rows, 0, unroll=4)

    loads["cot"].wait()
    pl.semaphore_wait(barrier, len(peers))

    for k in range(PARTS):
        go(cores.at[k], corer.at[k], at_core, "core", ("core", k))

    def to_other(first, rows):
        mine = cotf.at[tp, pl.ds(first, rows)]
        go(mine, mine, at_zh, "cot", "cot_z")

    to_other(0, 512)

    def to_near(half, h, d, key):
        mine = cotf.at[half * 4 + y, halves[h]]
        go(mine, mine, near_dev[d], "cot", key)

    def to_far(half, d, key):
        part = cotf.at[block_of(half, (3, 1)[d]), halves[d]]
        go(part, part, near_dev[d], "cot", key)

    for d in range(2):
        to_near(zh, d, d, "first")
    store_row(sqs, to_row(acc[...]))
    for d in (1, 2, 3):
        go(sqs, sqr.at[d - 1], at_y(d), "sq_y", "sq_y")
    loads["w"].wait()

    def weights(target):
        first = pl.ds(pl.multiple_of(((1 - zh) * 4 + target) * L, L), L)
        second = pl.ds(pl.multiple_of((zh * 4 + target) * L, L), L)
        return jnp.concatenate([w_v[:, first], w_v[:, second]], axis=1)

    def project(rows, cols):
        return jnp.dot(xg[rows, :], cols, preferred_element_type=F32)

    def send_far(d, q):
        go(pf.at[q, halves[d]], ar.at[d, q], near_dev[d], "proj", ("far", q))

    def send_near(d, q):
        go(pn.at[d, q, halves[1 - d]], cr.at[d, q], near_dev[d], "proj", ("near", q))

    def send_onward(q):
        arrived(("far", q), pf.at[q])
        for d in range(2):
            pn[d, q, halves[d], :] = (
                pn[d, q, halves[d], :].astype(F32) + ar[d, q].astype(F32)
            ).astype(BF)
            go(pn.at[d, q, halves[d]], br.at[d, q], near_dev[d], "proj", ("near", q))

    def add_own(k):
        arrived(("core", k), corer.at[k])
        for d in offsets:
            xi = (xx + d) % 4

            def add_partner(zi, carry, k=k, xi=xi):
                both = decoded(zi * 8 + xi * 2 + c, k) + corer[k, xi, zi].astype(F32)
                xs[k, xi, zi] = both.astype(BF)
                return carry
            lax.fori_loop(0, 4, add_partner, 0, unroll=4)
            if d:
                go(xs.at[k, xi], xr.at[k, d - 1], at_x(d), "x", ("x", k))

    cols = weights((y + 2) % 4)
    for d in range(2):
        value = project(halves[d], cols)
        for q in range(2):
            pf[q, halves[d], :] = value[:, q * L:(q + 1) * L].astype(BF)
        send_far(d, 0)
    add_own(0)
    add_own(1)
    for d in range(2):
        cols = weights((y + (1, 3)[d]) % 4)
        for h in (1 - d, d):
            value = project(halves[h], cols)
            for q in range(2):
                pn[d, q, halves[h], :] = value[:, q * L:(q + 1) * L].astype(BF)
            if h == 1 - d:
                send_near(d, 0)
    add_own(2)
    add_own(3)

    cols = weights(y)
    for h in range(2):
        value = project(halves[h], cols)
        for q in range(2):
            pown[q, halves[h], :] = value[:, q * L:(q + 1) * L]

    send_onward(0)
    for d in range(2):
        send_far(d, 1)
    for d in range(2):
        send_near(d, 1)

    arrived("sq_y", sqr)
    sqz[...] = sqs[...] + sqr[0] + sqr[1] + sqr[2]
    go(sqz, sqzr, at_zh, "sq_z", "sq_z")

    def along_x(k):
        arrived(("x", k), xr.at[k])

        def add(zi, carry, k=k):
            total = xs[k, xx, zi].astype(F32)
            for s in range(3):
                total = total + xr[k, s, zi].astype(F32)
            zs[k, zi] = total.astype(BF)
            return carry
        lax.fori_loop(0, 4, add, 0, unroll=4)
        for d in (2, 1, 3):
            go(zs.at[k, (zl + d) % 4], zr.at[k, d - 1], at_z(d), "z", ("z", k))

    def outer(k):
        arrived(("z", k), zr.at[k])
        total = zs[k, zl].astype(F32)
        for s in range(3):
            total = total + zr[k, s].astype(F32)
        delta = total * (1.0 / 32.0)
        part = columns_of(k)
        new_momentum = outer_push * mom_v[:, part] + delta
        new_global = glob_v[:, part] - outer_rate * (delta + outer_push * new_momentum)
        nm[:, part] = new_momentum
        ng[:, part] = new_global
        sh[k, c, xx, zl] = new_global.astype(BF)
        here = sh.at[k, c, xx, zl]
        for d in (2, 1, 3):
            go(here, here, at_z(d), "z_back", ("z_back", k))

    def spread_x(k):
        arrived(("z_back", k), zr.at[k])
        here = sh.at[k, c, xx]
        for d in (2, 1, 3):
            go(here, here, at_x(d), "x_back", ("x_back", k))

    def spread_core(k):
        arrived(("x_back", k), xr.at[k])
        go(sh.at[k, c], sh.at[k, c], at_core, "core_back", ("core_back", k))

    def transpose_part(j):
        xgt[pl.ds(j * 256, 256), :] = jnp.transpose(xg[:, pl.ds(j * 256, 256)])

    def send_proj(first, rows):
        part = zsend.at[pl.ds(first, rows)]
        go(part, zrecv.at[pl.ds(first, rows)], at_zh, "proj_z", "proj_z")

    def gather_part(q):
        arrived(("near", q), pf)
        for h in range(2):
            total = pown[q, halves[h], :] + br[h, q].astype(F32) + cr[1 - h, q].astype(F32)
            pown[q, halves[h], :] = total
            if q == 0:
                zsend[halves[h], :] = total.astype(BF)

    def weight_grad(blocks):
        for block in blocks:
            csf[block] = (cotf[block].astype(F32) * invb[...]).astype(BF)
        for i in range(0, len(blocks), 2):
            some = blocks[i:i + 2]
            right = jnp.concatenate([csf[block] for block in some], axis=1)
            value = jnp.dot(xgt[...], right, preferred_element_type=F32)
            for at, block in enumerate(some):
                gw[block] = value[:, at * L:(at + 1) * L]

    def normed_part(blocks, j):
        left = jnp.concatenate([cotf[block] for block in blocks], axis=1)
        rows = pl.ds(pl.multiple_of(j * 256, 256), 256)
        right = jnp.concatenate(
            [w_v[rows, pl.ds(pl.multiple_of(block * L, L), L)] for block in blocks], axis=1
        )
        return lax.dot_general(left, right, (((1,), (1,)), ((), ())), preferred_element_type=F32)

    def normed_grad(blocks, add):
        def keep_part(j, carry):
            value = normed_part(blocks, j)
            gn[j] = gn[j] + value if add else value
            return carry
        lax.fori_loop(0, 4, keep_part, 0)

    def finish_w(m):
        half = half_of(m)

        def block(b, carry):
            rows = pl.ds(pl.multiple_of(b * 32, 32), 32)
            part = pl.ds(pl.multiple_of(half * H, H), H)
            step = jnp.concatenate([gw[half * 4 + j, rows, :] for j in range(4)], axis=1)
            shared = jnp.concatenate([sh[2 * m + i, b % 2, (b // 2) % 4, b // 8] for i in range(2)], axis=1)
            mixed = (
                keep_share * w_v[rows, part].astype(F32)
                + (1.0 - keep_share) * shared.astype(F32)
                - (inner_rate * FACTOR) * step
            )
            nl[rows, part] = mixed.astype(BF)
            return carry
        lax.fori_loop(0, 32, block, 0, unroll=4)

    along_x(0)
    to_other(512, 256)
    for j in range(4):
        transpose_part(j)
    along_x(1)
    to_other(768, 256)
    normed_grad([tp], False)
    loads["glob"].wait()
    loads["mom"].wait()
    outer(0)
    along_x(2)

    gather_part(0)
    outer(1)

    send_onward(1)
    for d in range(2):
        to_near(zh, 1 - d, d, "rest")
    arrived("first", cotf.at[0])
    for d in range(2):
        to_far(zh, d, "rest")

    along_x(3)
    spread_x(0)
    outer(2)

    arrived("sq_z", sqzr)
    squares = row_of(sqz) + row_of(sqzr)
    inverse = lax.rsqrt(squares * (1.0 / D) + epsilon)
    invb[...] = to_column(inverse)
    spread_x(1)
    arrived("cot_z", cotf.at[other])
    acc[...] = pown[0] * cotf[other].astype(F32)
    weight_grad([tp, other])

    outer(3)
    send_proj(0, 256)

    gather_part(1)
    acc[...] = acc[...] + pown[1] * cotf[tp].astype(F32)
    store_row(ins, to_row(acc[...]))
    for d in (1, 2, 3):
        go(ins, inr.at[d - 1], at_y(d), "in_y", "in_y")
    for d in range(2):
        to_near(1 - zh, d, d, "other_first")
    for d in range(2):
        to_near(1 - zh, 1 - d, d, "other_second")

    spread_x(2)
    spread_core(0)

    spread_x(3)
    send_proj(256, 256)
    spread_core(1)

    arrived("rest", cotf.at[pl.ds(0, 2)])
    near_blocks = [block_of(zh, d) for d in (1, 3)]
    normed_grad([other] + near_blocks + [block_of(zh, 2)], True)

    arrived("other_first", cotf.at[0])
    for d in range(2):
        to_far(1 - zh, d, "other_far")
    arrived("in_y", inr)
    inz[...] = ins[...] + inr[0] + inr[1] + inr[2]
    go(inz, inzr, at_zh, "in_z", "in_z")
    send_proj(512, 512)

    spread_core(2)
    weight_grad(near_blocks + [block_of(zh, 2)])
    spread_core(3)
    for k in (0, 1):
        arrived(("core_back", k), corer.at[k])
    finish_w(0)

    arrived("other_second", cotf.at[0])
    near_blocks = [block_of(1 - zh, d) for d in (1, 3)]
    normed_grad(near_blocks, True)
    arrived("in_z", inzr)
    inner = row_of(inz) + row_of(inzr)
    coefb[...] = to_column(inverse * inverse * inverse * inner * (FACTOR / D))
    weight_grad(near_blocks)
    arrived("other_far", cotf.at[0])
    last = [block_of(1 - zh, 2)]

    def finish_x(j, carry):
        part = pl.ds(pl.multiple_of(j * 256, 256), 256)
        value = (gn[j] + normed_part(last, j)) * (gain_v[:, part] * FACTOR)
        scale = jnp.concatenate([invb[...]] * 2, axis=1)
        coef = jnp.concatenate([coefb[...]] * 2, axis=1)
        gx[:, part] = (value * scale - x_v[:, part].astype(F32) * coef).astype(BF)
        return carry
    lax.fori_loop(0, 4, finish_x, 0)

    weight_grad(last)
    arrived("proj_z", zrecv)
    proj[...] = ((pown[1] + zrecv[...].astype(F32)) * invb[...] * FACTOR).astype(BF)
    for k in (2, 3):
        arrived(("core_back", k), corer.at[k])
    finish_w(1)

    departed("cot", cotf.at[pl.ds(0, 7)])
    departed("proj", cotf.at[pl.ds(0, 6)])
    departed("proj_z", zsend)
    departed("x", xr)
    departed("z", zr)
    departed("z_back", zr)
    departed("x_back", xr)
    departed("core", cores)
    departed("core_back", cores)
    departed("sq_y", sqr)
    departed("in_y", inr)
    departed("sq_z", sqz)
    departed("in_z", inz)
    assert max(len(used) for used in slots.values()) <= SEMS


def writer(*refs):
    sources, targets, sem = refs[:5], refs[5:10], refs[10]
    copies = [pltpu.make_async_copy(s, t, sem.at[i]) for i, (s, t) in enumerate(zip(sources, targets))]
    for copy in copies:
        copy.start()
    for copy in copies:
        copy.wait()


def local(
    tokens_in, gain, cotangent, local_weight, packed_codes, code_scales, global_weight, momentum
):
    any_ = pl.BlockSpec(memory_space=pltpu.HBM)
    vm = pltpu.VMEM
    shapes = (((T, L), BF), ((T, F), BF), ((F, C), BF), ((32, C), F32), ((32, C), F32))
    results = pl.pallas_call(
        kernel,
        out_shape=tuple(vm(*shape) for shape in shapes),
        in_specs=[any_] * 8,
        out_specs=[pl.BlockSpec(memory_space=vm)] * 5,
        scratch_shapes=[
            vm((T, F), BF), vm((1, F), F32), vm((F, C), BF), vm((F, C // 2), jnp.int32), vm((8, F), F32), vm((2, F, 4), F32),
            vm((32, C), F32), vm((32, C), F32),
            vm((T, F), BF), vm((F, T), BF), vm((8, T, L), BF), vm((8, T, L), BF),
            vm((2, T, L), BF), vm((2, 2, T, L), BF), vm((2, T, L), F32),
            vm((2, 2, H, L), BF), vm((2, 2, H, L), BF), vm((2, 2, H, L), BF),
            vm((T, L), BF), vm((T, L), BF),
            vm((PARTS, 4, 4, 32, Q), BF), vm((PARTS, 4, 4, 32, Q), BF), vm((PARTS, 4, 4, 32, Q), BF),
            vm((PARTS, 3, 4, 32, Q), BF), vm((PARTS, 4, 32, Q), BF), vm((PARTS, 3, 32, Q), BF), vm((8, L), F32),
            vm((PARTS, 2, 4, 4, 32, Q), BF),
            vm((T, L), F32), vm((T, L), F32), vm((T, L), F32),
            vm((8, L), F32), vm((3, 8, L), F32), vm((8, L), F32), vm((8, L), F32),
            vm((8, L), F32), vm((3, 8, L), F32), vm((8, L), F32), vm((8, L), F32),
            vm((4, T, 256), F32), vm((8, F, L), F32),
            pltpu.SemaphoreType.DMA((SEMS,)), pltpu.SemaphoreType.DMA((SEMS,)),
            pltpu.SemaphoreType.DMA((8,)),
        ],
        compiler_params=pltpu.CompilerParams(
            collective_id=0, has_side_effects=True, vmem_limit_bytes=48 * 2**20
        ),
        cost_estimate=pl.CostEstimate(flops=6 * 2**30, bytes_accessed=12 * 2**20, transcendentals=0),
    )(*(
        pltpu.with_memory_space_constraint(arg, pltpu.HBM) for arg in (
            tokens_in, gain.reshape(1, F), cotangent, local_weight[0], packed_codes[0], code_scales[0].T,
            global_weight[0], momentum[0],
        )
    ))
    projected, grad_x, new_local, new_global, new_momentum = pl.pallas_call(
        writer,
        out_shape=tuple(jax.ShapeDtypeStruct(*shape) for shape in shapes),
        in_specs=[pl.BlockSpec(memory_space=vm)] * 5,
        out_specs=[any_] * 5,
        scratch_shapes=[pltpu.SemaphoreType.DMA((5,))],
        compiler_params=pltpu.CompilerParams(vmem_limit_bytes=8 * 2**20),
    )(*results)
    return (projected, grad_x, new_local[None], new_global[None], new_momentum[None])


def solution(mesh):
    return jax.shard_map(
        local,
        mesh=mesh,
        in_specs=(
            P("rep", "tp"),
            P("tp"),
            P("rep", "tp"),
            P("rep", "tp", None),
            P("rep", "tp", None),
            P("rep", "tp", None),
            P("tp", "rep", None),
            P("tp", "rep", None),
        ),
        out_specs=(
            P("rep", "tp"),
            P("rep", "tp"),
            P("rep", "tp", None),
            P("tp", "rep", None),
            P("tp", "rep", None),
        ),
        check_vma=False,
    )
```

```python
import math

import jax
import jax.numpy as jnp
from jax import lax
from jax.experimental import pallas as pl
from jax.experimental.pallas import tpu as pltpu
from jax.sharding import PartitionSpec as P

MESH = pl.DeviceIdType.MESH
BF = jnp.bfloat16
F32 = jnp.float32

D = 8192
T = 1024
F = 1024
C = 1024
H = 512
Q = 256
PARTS = 4
L = 128
FACTOR = 1.0 / math.sqrt(D)

epsilon = 1e-05
outer_rate = 0.7
outer_push = 0.9
keep_share = 0.5
inner_rate = 0.5

SEMS = 48


def row_of(ref):
    return jnp.concatenate([ref[pl.ds(i, 1), :] for i in range(8)], axis=1)


def store_row(ref, row):
    for i in range(8):
        ref[pl.ds(i, 1), :] = row[:, i * L:(i + 1) * L]


def to_row(column_sums):
    return jnp.sum(jnp.transpose(column_sums), axis=0, keepdims=True)


def to_column(row):
    return jnp.transpose(jnp.broadcast_to(row, (L, T)))


def kernel(
    x_hbm, gain_hbm, cot_hbm, w_hbm, codes_hbm, scales_hbm, glob_hbm, mom_hbm,
    proj, gx, nl, ng, nm,
    x_v, gain_v, w_v, codes_v, scalest_v, scales_v, glob_v, mom_v,
    xg, xgt, cotf, csf, pf, pn, pown, ar, br, cr, zsend, zrecv,
    cores, corer, xs, xr, zs, zr, zown, sh,
    acc, invb, coefb, sqs, sqr, sqz, sqzr, ins, inr, inz, inzr,
    gn, gw,
    send_sem, recv_sem, load_sem,
):
    rep = lax.axis_index("rep")
    tp = lax.axis_index("tp")
    zl = rep // 8
    xx = (rep // 2) % 4
    c = rep % 2
    zh = tp // 4
    y = tp % 4

    def at_y(d):
        return (rep, zh * 4 + (y + d) % 4)

    def at_x(d):
        return (zl * 8 + ((xx + d) % 4) * 2 + c, tp)

    def at_z(d):
        return (((zl + d) % 4) * 8 + xx * 2 + c, tp)

    at_zh = (rep, (1 - zh) * 4 + y)
    at_core = (zl * 8 + xx * 2 + (1 - c), tp)

    slots = {"send": {}, "recv": {}}

    def slot(kind, key):
        return slots[kind].setdefault(key, len(slots[kind]))

    def describe(src, dst, dev, send_key, recv_key):
        return pltpu.make_async_remote_copy(
            src_ref=src, dst_ref=dst,
            send_sem=send_sem.at[slot("send", send_key)], recv_sem=recv_sem.at[slot("recv", recv_key)],
            device_id=dev, device_id_type=MESH,
        )

    def go(src, dst, dev, send_key, recv_key):
        describe(src, dst, dev, send_key, recv_key).start()

    def arrived(recv_key, like):
        describe(like, like, at_core, "none", recv_key).wait_recv()

    def departed(send_key, like):
        describe(like, like, at_core, send_key, "none").wait_send()

    loads = {}
    for i, (name, src, dst) in enumerate((
        ("scales", scales_hbm, scalest_v), ("codes", codes_hbm, codes_v),
        ("cot", cot_hbm, cotf.at[tp]), ("gain", gain_hbm, gain_v), ("x", x_hbm, x_v),
        ("w", w_hbm, w_v), ("glob", glob_hbm, glob_v), ("mom", mom_hbm, mom_v),
    )):
        loads[name] = pltpu.make_async_copy(src, dst, load_sem.at[i])
        loads[name].start()

    barrier = pltpu.get_barrier_semaphore()
    peers = [at_y(1), at_y(2), at_y(3), at_zh, at_core]
    peers += [at_x(d) for d in (1, 2, 3)] + [at_z(d) for d in (1, 2, 3)]
    for dev in peers:
        pl.semaphore_signal(barrier, inc=1, device_id=dev, device_id_type=MESH)

    def half_of(m):
        return zh if m == 0 else 1 - zh

    def columns_of(k):
        return pl.ds(pl.multiple_of(half_of(k // 2) * H + (k % 2) * Q, Q), Q)

    def decoded(block, k):
        rows = pl.ds(pl.multiple_of(block * 32, 32), 32)
        words = codes_v[rows, pl.ds((k % 2) * Q, Q)]
        codes = (jnp.bitwise_and(jnp.right_shift(words, 4 * half_of(k // 2)), 15) - 8).astype(F32)
        scales = scales_v[k // 2, rows, :]
        return jnp.concatenate(
            [codes[:, g * L:(g + 1) * L] * scales[:, (k % 2) * 2 + g:(k % 2) * 2 + g + 1] for g in range(2)],
            axis=1,
        )

    offsets = (2, 1, 3, 0)
    near_dev = (at_y(1), at_y(3))
    halves = (pl.ds(0, H), pl.ds(H, H))
    other = (1 - zh) * 4 + y

    def block_of(half, d):
        return half * 4 + (y + d) % 4

    loads["scales"].wait()
    all_scales = jnp.transpose(scalest_v[...])
    first, second = all_scales[:, 0:4], all_scales[:, 4:8]
    scales_v[0] = jnp.where(zh == 0, first, second)
    scales_v[1] = jnp.where(zh == 0, second, first)
    loads["codes"].wait()
    for k in range(PARTS):
        def for_partner(i, carry, k=k):
            cores[k, i // 4, i % 4] = decoded((i % 4) * 8 + (i // 4) * 2 + (1 - c), k).astype(BF)
            return carry
        lax.fori_loop(0, 16, for_partner, 0, unroll=4)

    loads["gain"].wait()
    loads["x"].wait()
    gain = gain_v[...]

    def scale_rows(i, carry):
        rows = pl.ds(pl.multiple_of(i * 32, 32), 32)
        wide = x_v[rows, :].astype(F32)
        xg[rows, :] = (wide * gain).astype(BF)
        squares = wide * wide
        total = squares[:, 0:L]
        for j in range(1, 8):
            total = total + squares[:, j * L:(j + 1) * L]
        acc[rows, :] = total
        return carry
    lax.fori_loop(0, 32, scale_rows, 0, unroll=4)

    loads["cot"].wait()
    pl.semaphore_wait(barrier, len(peers))

    for k in range(PARTS):
        go(cores.at[k], corer.at[k], at_core, "core", ("core", k))

    def to_other(first, rows):
        mine = cotf.at[tp, pl.ds(first, rows)]
        go(mine, mine, at_zh, "cot", "cot_z")

    to_other(0, 512)

    def to_near(half, h, d, key):
        mine = cotf.at[half * 4 + y, halves[h]]
        go(mine, mine, near_dev[d], "cot", key)

    def to_far(half, d, key):
        part = cotf.at[block_of(half, (3, 1)[d]), halves[d]]
        go(part, part, near_dev[d], "cot", key)

    for d in range(2):
        to_near(zh, d, d, "first")
    store_row(sqs, to_row(acc[...]))
    for d in (1, 2, 3):
        go(sqs, sqr.at[d - 1], at_y(d), "sq_y", "sq_y")
    loads["w"].wait()

    def weights(target):
        first = pl.ds(pl.multiple_of(((1 - zh) * 4 + target) * L, L), L)
        second = pl.ds(pl.multiple_of((zh * 4 + target) * L, L), L)
        return jnp.concatenate([w_v[:, first], w_v[:, second]], axis=1)

    def project(rows, cols):
        return jnp.dot(xg[rows, :], cols, preferred_element_type=F32)

    def send_far(d, q):
        go(pf.at[q, halves[d]], ar.at[d, q], near_dev[d], "proj", ("far", q))

    def send_near(d, q):
        go(pn.at[d, q, halves[1 - d]], cr.at[d, q], near_dev[d], "proj", ("near", q))

    def send_onward(q):
        arrived(("far", q), pf.at[q])
        for d in range(2):
            pn[d, q, halves[d], :] = (
                pn[d, q, halves[d], :].astype(F32) + ar[d, q].astype(F32)
            ).astype(BF)
            go(pn.at[d, q, halves[d]], br.at[d, q], near_dev[d], "proj", ("near", q))

    def add_own(k):
        arrived(("core", k), corer.at[k])
        for d in offsets:
            xi = (xx + d) % 4

            def add_partner(zi, carry, k=k, xi=xi):
                both = decoded(zi * 8 + xi * 2 + c, k) + corer[k, xi, zi].astype(F32)
                xs[k, xi, zi] = both.astype(BF)
                return carry
            lax.fori_loop(0, 4, add_partner, 0, unroll=4)
            if d:
                go(xs.at[k, xi], xr.at[k, d - 1], at_x(d), "x", ("x", k))

    cols = weights((y + 2) % 4)
    for d in range(2):
        value = project(halves[d], cols)
        for q in range(2):
            pf[q, halves[d], :] = value[:, q * L:(q + 1) * L].astype(BF)
        send_far(d, 0)
    add_own(0)
    add_own(1)
    for d in range(2):
        cols = weights((y + (1, 3)[d]) % 4)
        for h in (1 - d, d):
            value = project(halves[h], cols)
            for q in range(2):
                pn[d, q, halves[h], :] = value[:, q * L:(q + 1) * L].astype(BF)
            if h == 1 - d:
                send_near(d, 0)
    add_own(2)
    add_own(3)

    cols = weights(y)
    for h in range(2):
        value = project(halves[h], cols)
        for q in range(2):
            pown[q, halves[h], :] = value[:, q * L:(q + 1) * L]

    send_onward(0)
    for d in range(2):
        send_far(d, 1)
    for d in range(2):
        send_near(d, 1)

    arrived("sq_y", sqr)
    sqz[...] = sqs[...] + sqr[0] + sqr[1] + sqr[2]
    go(sqz, sqzr, at_zh, "sq_z", "sq_z")

    def along_x(k):
        arrived(("x", k), xr.at[k])

        def add(zi, carry, k=k):
            total = xs[k, xx, zi].astype(F32)
            for s in range(3):
                total = total + xr[k, s, zi].astype(F32)
            zs[k, zi] = total.astype(BF)
            return carry
        lax.fori_loop(0, 4, add, 0, unroll=4)
        for d in (2, 1, 3):
            go(zs.at[k, (zl + d) % 4], zr.at[k, d - 1], at_z(d), "z", ("z", k))

    def outer(k):
        arrived(("z", k), zr.at[k])
        total = zs[k, zl].astype(F32)
        for s in range(3):
            total = total + zr[k, s].astype(F32)
        delta = total * (1.0 / 32.0)
        part = columns_of(k)
        new_momentum = outer_push * mom_v[:, part] + delta
        new_global = glob_v[:, part] - outer_rate * (delta + outer_push * new_momentum)
        nm[:, part] = new_momentum
        ng[:, part] = new_global
        sh[k, c, xx, zl] = new_global.astype(BF)
        here = sh.at[k, c, xx, zl]
        for d in (2, 1, 3):
            go(here, here, at_z(d), "z_back", ("z_back", k))

    def spread_x(k):
        arrived(("z_back", k), zr.at[k])
        here = sh.at[k, c, xx]
        for d in (2, 1, 3):
            go(here, here, at_x(d), "x_back", ("x_back", k))

    def spread_core(k):
        arrived(("x_back", k), xr.at[k])
        go(sh.at[k, c], sh.at[k, c], at_core, "core_back", ("core_back", k))

    def transpose_part(j):
        xgt[pl.ds(j * 256, 256), :] = jnp.transpose(xg[:, pl.ds(j * 256, 256)])

    def send_proj(first, rows):
        part = zsend.at[pl.ds(first, rows)]
        go(part, zrecv.at[pl.ds(first, rows)], at_zh, "proj_z", "proj_z")

    def gather_part(q):
        arrived(("near", q), pf)
        for h in range(2):
            total = pown[q, halves[h], :] + br[h, q].astype(F32) + cr[1 - h, q].astype(F32)
            pown[q, halves[h], :] = total
            if q == 0:
                zsend[halves[h], :] = total.astype(BF)

    def weight_grad(blocks):
        for block in blocks:
            csf[block] = (cotf[block].astype(F32) * invb[...]).astype(BF)
        for i in range(0, len(blocks), 2):
            some = blocks[i:i + 2]
            right = jnp.concatenate([csf[block] for block in some], axis=1)
            value = jnp.dot(xgt[...], right, preferred_element_type=F32)
            for at, block in enumerate(some):
                gw[block] = value[:, at * L:(at + 1) * L]

    def normed_part(blocks, j):
        left = jnp.concatenate([cotf[block] for block in blocks], axis=1)
        rows = pl.ds(pl.multiple_of(j * 256, 256), 256)
        right = jnp.concatenate(
            [w_v[rows, pl.ds(pl.multiple_of(block * L, L), L)] for block in blocks], axis=1
        )
        return lax.dot_general(left, right, (((1,), (1,)), ((), ())), preferred_element_type=F32)

    def normed_grad(blocks, add):
        def keep_part(j, carry):
            value = normed_part(blocks, j)
            gn[j] = gn[j] + value if add else value
            return carry
        lax.fori_loop(0, 4, keep_part, 0)

    def finish_w(m):
        half = half_of(m)

        def block(b, carry):
            rows = pl.ds(pl.multiple_of(b * 32, 32), 32)
            part = pl.ds(pl.multiple_of(half * H, H), H)
            step = jnp.concatenate([gw[half * 4 + j, rows, :] for j in range(4)], axis=1)
            shared = jnp.concatenate([sh[2 * m + i, b % 2, (b // 2) % 4, b // 8] for i in range(2)], axis=1)
            mixed = (
                keep_share * w_v[rows, part].astype(F32)
                + (1.0 - keep_share) * shared.astype(F32)
                - (inner_rate * FACTOR) * step
            )
            nl[rows, part] = mixed.astype(BF)
            return carry
        lax.fori_loop(0, 32, block, 0, unroll=4)

    along_x(0)
    to_other(512, 256)
    for j in range(4):
        transpose_part(j)
    along_x(1)
    to_other(768, 256)
    normed_grad([tp], False)
    loads["glob"].wait()
    loads["mom"].wait()
    outer(0)
    along_x(2)

    gather_part(0)
    outer(1)

    send_onward(1)
    for d in range(2):
        to_near(zh, 1 - d, d, "rest")
    arrived("first", cotf.at[0])
    for d in range(2):
        to_far(zh, d, "rest")

    along_x(3)
    spread_x(0)
    outer(2)

    arrived("sq_z", sqzr)
    squares = row_of(sqz) + row_of(sqzr)
    inverse = lax.rsqrt(squares * (1.0 / D) + epsilon)
    invb[...] = to_column(inverse)
    spread_x(1)
    arrived("cot_z", cotf.at[other])
    acc[...] = pown[0] * cotf[other].astype(F32)
    weight_grad([tp, other])

    outer(3)
    send_proj(0, 128)

    gather_part(1)
    acc[...] = acc[...] + pown[1] * cotf[tp].astype(F32)
    store_row(ins, to_row(acc[...]))
    for d in (1, 2, 3):
        go(ins, inr.at[d - 1], at_y(d), "in_y", "in_y")
    for d in range(2):
        to_near(1 - zh, d, d, "other_first")
    for d in range(2):
        to_near(1 - zh, 1 - d, d, "other_second")

    spread_x(2)
    spread_core(0)

    spread_x(3)
    send_proj(128, 384)
    spread_core(1)

    arrived("rest", cotf.at[pl.ds(0, 2)])
    near_blocks = [block_of(zh, d) for d in (1, 3)]
    normed_grad([other] + near_blocks + [block_of(zh, 2)], True)

    arrived("other_first", cotf.at[0])
    for d in range(2):
        to_far(1 - zh, d, "other_far")
    arrived("in_y", inr)
    inz[...] = ins[...] + inr[0] + inr[1] + inr[2]
    go(inz, inzr, at_zh, "in_z", "in_z")
    send_proj(512, 512)

    spread_core(2)
    weight_grad(near_blocks + [block_of(zh, 2)])
    spread_core(3)
    for k in (0, 1):
        arrived(("core_back", k), corer.at[k])
    finish_w(0)

    arrived("other_second", cotf.at[0])
    near_blocks = [block_of(1 - zh, d) for d in (1, 3)]
    normed_grad(near_blocks, True)
    arrived("in_z", inzr)
    inner = row_of(inz) + row_of(inzr)
    coefb[...] = to_column(inverse * inverse * inverse * inner * (FACTOR / D))
    weight_grad(near_blocks)
    arrived("other_far", cotf.at[0])
    last = [block_of(1 - zh, 2)]

    def finish_x(j, carry):
        part = pl.ds(pl.multiple_of(j * 256, 256), 256)
        value = (gn[j] + normed_part(last, j)) * (gain_v[:, part] * FACTOR)
        scale = jnp.concatenate([invb[...]] * 2, axis=1)
        coef = jnp.concatenate([coefb[...]] * 2, axis=1)
        gx[:, part] = (value * scale - x_v[:, part].astype(F32) * coef).astype(BF)
        return carry
    lax.fori_loop(0, 4, finish_x, 0)

    weight_grad(last)
    arrived("proj_z", zrecv)
    proj[...] = ((pown[1] + zrecv[...].astype(F32)) * invb[...] * FACTOR).astype(BF)
    for k in (2, 3):
        arrived(("core_back", k), corer.at[k])
    finish_w(1)

    departed("cot", cotf.at[pl.ds(0, 7)])
    departed("proj", cotf.at[pl.ds(0, 6)])
    departed("proj_z", zsend)
    departed("x", xr)
    departed("z", zr)
    departed("z_back", zr)
    departed("x_back", xr)
    departed("core", cores)
    departed("core_back", cores)
    departed("sq_y", sqr)
    departed("in_y", inr)
    departed("sq_z", sqz)
    departed("in_z", inz)
    assert max(len(used) for used in slots.values()) <= SEMS


def writer(*refs):
    sources, targets, sem = refs[:5], refs[5:10], refs[10]
    copies = [pltpu.make_async_copy(s, t, sem.at[i]) for i, (s, t) in enumerate(zip(sources, targets))]
    for copy in copies:
        copy.start()
    for copy in copies:
        copy.wait()


def local(
    tokens_in, gain, cotangent, local_weight, packed_codes, code_scales, global_weight, momentum
):
    any_ = pl.BlockSpec(memory_space=pltpu.HBM)
    vm = pltpu.VMEM
    shapes = (((T, L), BF), ((T, F), BF), ((F, C), BF), ((32, C), F32), ((32, C), F32))
    results = pl.pallas_call(
        kernel,
        out_shape=tuple(vm(*shape) for shape in shapes),
        in_specs=[any_] * 8,
        out_specs=[pl.BlockSpec(memory_space=vm)] * 5,
        scratch_shapes=[
            vm((T, F), BF), vm((1, F), F32), vm((F, C), BF), vm((F, C // 2), jnp.int32), vm((8, F), F32), vm((2, F, 4), F32),
            vm((32, C), F32), vm((32, C), F32),
            vm((T, F), BF), vm((F, T), BF), vm((8, T, L), BF), vm((8, T, L), BF),
            vm((2, T, L), BF), vm((2, 2, T, L), BF), vm((2, T, L), F32),
            vm((2, 2, H, L), BF), vm((2, 2, H, L), BF), vm((2, 2, H, L), BF),
            vm((T, L), BF), vm((T, L), BF),
            vm((PARTS, 4, 4, 32, Q), BF), vm((PARTS, 4, 4, 32, Q), BF), vm((PARTS, 4, 4, 32, Q), BF),
            vm((PARTS, 3, 4, 32, Q), BF), vm((PARTS, 4, 32, Q), BF), vm((PARTS, 3, 32, Q), BF), vm((8, L), F32),
            vm((PARTS, 2, 4, 4, 32, Q), BF),
            vm((T, L), F32), vm((T, L), F32), vm((T, L), F32),
            vm((8, L), F32), vm((3, 8, L), F32), vm((8, L), F32), vm((8, L), F32),
            vm((8, L), F32), vm((3, 8, L), F32), vm((8, L), F32), vm((8, L), F32),
            vm((4, T, 256), F32), vm((8, F, L), F32),
            pltpu.SemaphoreType.DMA((SEMS,)), pltpu.SemaphoreType.DMA((SEMS,)),
            pltpu.SemaphoreType.DMA((8,)),
        ],
        compiler_params=pltpu.CompilerParams(
            collective_id=0, has_side_effects=True, vmem_limit_bytes=48 * 2**20
        ),
        cost_estimate=pl.CostEstimate(flops=6 * 2**30, bytes_accessed=12 * 2**20, transcendentals=0),
    )(*(
        pltpu.with_memory_space_constraint(arg, pltpu.HBM) for arg in (
            tokens_in, gain.reshape(1, F), cotangent, local_weight[0], packed_codes[0], code_scales[0].T,
            global_weight[0], momentum[0],
        )
    ))
    projected, grad_x, new_local, new_global, new_momentum = pl.pallas_call(
        writer,
        out_shape=tuple(jax.ShapeDtypeStruct(*shape) for shape in shapes),
        in_specs=[pl.BlockSpec(memory_space=vm)] * 5,
        out_specs=[any_] * 5,
        scratch_shapes=[pltpu.SemaphoreType.DMA((5,))],
        compiler_params=pltpu.CompilerParams(vmem_limit_bytes=8 * 2**20),
    )(*results)
    return (projected, grad_x, new_local[None], new_global[None], new_momentum[None])


def solution(mesh):
    return jax.shard_map(
        local,
        mesh=mesh,
        in_specs=(
            P("rep", "tp"),
            P("tp"),
            P("rep", "tp"),
            P("rep", "tp", None),
            P("rep", "tp", None),
            P("rep", "tp", None),
            P("tp", "rep", None),
            P("tp", "rep", None),
        ),
        out_specs=(
            P("rep", "tp"),
            P("rep", "tp"),
            P("rep", "tp", None),
            P("tp", "rep", None),
            P("tp", "rep", None),
        ),
        check_vma=False,
    )
```
